256 devices in a mesh: row: 32 (over y, x, core), col: 8 (over z).
Axes of the slice: x: 4, y: 4, z: 8, core: 2. Of those that a mesh axis runs over, the one named last changes fastest.
Arguments:
- root_inv: float32 [4096, 4096], P('row', 'col'), as said below
- level1_inv: float32 [1024, 2, 1024], P('row', None, 'col'), as said below
- level1_panel: float32 [4096, 2, 1024], P('row', None, 'col'), may hold values from -0.0625 to 0.0625
- child_inv: float32 [4, 1024, 1024], P(None, 'row', 'col'), as said below
- child_panel: float32 [4, 2048, 1024], P(None, 'row', 'col'), may hold values from -0.09375 to 0.09375
- child_width: int32 [4], replicated, may hold values from 1 to 1024, 2560 in all
- child_parent: int32 [4], replicated, may hold values from 0 to 1, as said below
- child_blocks: int32 [4, 64], replicated, may hold values from 0 to 159, as said below
Outputs:
- leverage_root: float32 [4096], P('row')
- leverage_parent: float32 [2, 1024], P(None, 'row')
- leverage_child: float32 [4, 1024], P(None, 'col')
The draws below stay inside these ranges and needn't reach their ends.
Inputs may be any that keep to these rules, and one draw needn't show every extreme that they name: `root_inv`: zero above the diagonal. `level1_inv`: each [:, k, :] is zero above the diagonal. `child_inv`: each [j] is zero above the diagonal. `child_width`: the widths sum to 2560. `child_parent`: each parent has exactly two of the 4 children. `child_blocks`: each row lists 64 distinct numbers in increasing order, 0 and 159 among them; numbers below 128 name blocks of the root, the others blocks of the supernode's parent.
All inputs are finite; a program needn't handle non-finite values.
Results may differ from the reference program's by a relative error of at most 0.0001.
Values sent between devices are 32-bit elements; how exact they have to be, the bound alone decides.
No kernel may reach another device: no remote copies, remote signals or barrier semaphores. Data moves between devices by JAX's collectives and lax.ppermute only.
A program may use at most 128 MiB of HBM per device.

```python
import math
import jax
import jax.numpy as jnp
import numpy as np
from jax import lax

ROOT_COLS = 4096
PARENT_COLS = 1024
CHILD_COLS = 1024
BLOCK_ROWS = 32
STRUCT_BLOCKS = 64
CHILDREN = 4
PARENTS = 2
WIDTH_TOTAL = 2560
ANCESTOR_BLOCKS = 160


def lower_factor(noise, diagonal, width):
    places = jnp.arange(width, dtype=jnp.int32)
    below = (places[:, None] > places[None, :]).astype(jnp.float32)
    unit = (places[:, None] == places[None, :]).astype(jnp.float32)
    return noise * below * (0.6 * width ** (-0.5)) + diagonal[..., None, :] * unit


def draw_root_inv(key, part):
    key = jax.random.fold_in(key, 11)
    first, second = jax.random.split(key, 2)
    shape = (ROOT_COLS, ROOT_COLS)
    noise = jax.random.normal(first, shape, jnp.float32)
    diagonal = 0.8 + 0.4 * jax.random.uniform(second, (ROOT_COLS,), jnp.float32)
    return lower_factor(noise, diagonal, ROOT_COLS)


def draw_level1_inv(key, part):
    key = jax.random.fold_in(key, 23)
    first, second = jax.random.split(key, 2)
    shape = (PARENTS, PARENT_COLS, PARENT_COLS)
    noise = jax.random.normal(first, shape, jnp.float32)
    diagonal = 0.8 + 0.4 * jax.random.uniform(second, (PARENTS, PARENT_COLS), jnp.float32)
    return jnp.transpose(lower_factor(noise, diagonal, PARENT_COLS), (1, 0, 2))


def draw_child_inv(key, part):
    key = jax.random.fold_in(key, 31)
    first, second = jax.random.split(key, 2)
    shape = (CHILDREN, CHILD_COLS, CHILD_COLS)
    noise = jax.random.normal(first, shape, jnp.float32)
    diagonal = 0.8 + 0.4 * jax.random.uniform(second, (CHILDREN, CHILD_COLS), jnp.float32)
    return lower_factor(noise, diagonal, CHILD_COLS)


def draw_child_parent(key, part):
    key = jax.random.fold_in(key, 41)
    order = jax.random.permutation(key, jnp.arange(CHILDREN, dtype=jnp.int32))
    return (order // 2).astype(jnp.int32)


def pick_blocks(key):
    inner = jax.random.permutation(key, jnp.arange(1, ANCESTOR_BLOCKS - 1, dtype=jnp.int32))[:STRUCT_BLOCKS - 2]
    ends = jnp.array([0, ANCESTOR_BLOCKS - 1], dtype=jnp.int32)
    return jnp.sort(jnp.concatenate([ends, inner])).astype(jnp.int32)


def draw_child_blocks(key, part):
    key = jax.random.fold_in(key, 53)
    return jax.vmap(pick_blocks)(jax.random.split(key, CHILDREN))


def levels(stream_key, extent, shards, smallest, high):
    def one(position, shards_of):
        draws = jax.random.uniform(jax.random.fold_in(jax.random.fold_in(stream_key, 6), position), (shards_of,), jnp.float32, smallest / len(shards), high / len(shards))
        return jnp.repeat(jnp.exp(draws), extent[position] // shards_of).reshape((-1,) + (1,) * (len(extent) - position - 1))

    loudness = one(*shards[0])
    for cut in shards[1:]:
        loudness = loudness * one(*cut)
    return loudness


def split_up(number_of, total, most, slope):
    portions = [(1 << 20) // math.isqrt(rank ** slope) + 1 for rank in range(2, number_of + 1)]
    rest, counts = total - most - (number_of - 1), [1] * (number_of - 1)
    while rest > 0:
        free = [i for i in range(number_of - 1) if counts[i] < most]
        whole, budget = sum([portions[i] for i in free]), rest
        for i in free:
            more = min(most - counts[i], max(1, budget * portions[i] // whole), rest)
            counts[i] = counts[i] + more
            rest = rest - more
    return np.array([most] + counts)


def ragged(stream_key, amount, total, reach, slope):
    if amount == 2:
        one = jax.random.randint(stream_key, (), max(1, total - reach), min(reach, total - 1) + 1)
        return jnp.stack([one, total - one])
    sizes = jnp.asarray(split_up(amount, total, reach, slope), jnp.int32)
    pairs = (amount - 1) // 2
    donor, taker = sizes[1:1 + 2 * pairs:2], sizes[2:2 + 2 * pairs:2]
    margin = jnp.minimum(donor - 1, reach - taker)
    shifted = jax.random.randint(jax.random.fold_in(stream_key, 1), (pairs,), 0, 1 << 20) % (margin + 1)
    sizes = sizes.at[1:1 + 2 * pairs:2].set(donor - shifted).at[2:2 + 2 * pairs:2].set(taker + shifted)
    return sizes[jax.random.permutation(jax.random.fold_in(stream_key, 2), amount)]


def normal_values(own_key, dims, deviation, most, pieces=(), held_as=jnp.bfloat16):
    values = deviation * jax.random.normal(own_key, dims, jnp.float32)
    if pieces:
        values = values * levels(own_key, dims, pieces, -0.22, 0.18)
    return jnp.clip(values, -most, most).astype(held_as)


def setup_inputs(seed: int = 0) -> dict:
    streams_of = jax.random.split(jax.random.key(seed), 9)
    root_inv = draw_root_inv(jax.random.fold_in(streams_of[8], 71), 0)
    level1_inv = draw_level1_inv(jax.random.fold_in(streams_of[8], 71), 0)
    level1_panel = normal_values(streams_of[2], (ROOT_COLS, PARENTS, PARENT_COLS), (2 * ROOT_COLS) ** -0.5, 0.0625, ((0, 32), (2, 8)), jnp.float32)
    child_inv = draw_child_inv(jax.random.fold_in(streams_of[8], 71), 0)
    child_panel = normal_values(streams_of[4], (CHILDREN, STRUCT_BLOCKS * BLOCK_ROWS, CHILD_COLS), (2 * STRUCT_BLOCKS * BLOCK_ROWS) ** -0.5, 0.09375, ((1, 32), (2, 8)), jnp.float32)
    child_width = ragged(streams_of[5], CHILDREN, WIDTH_TOTAL, CHILD_COLS, 1).astype(jnp.int32)
    child_parent = draw_child_parent(jax.random.fold_in(streams_of[8], 71), 0)
    child_blocks = draw_child_blocks(jax.random.fold_in(streams_of[8], 71), 0)
    return dict(root_inv=root_inv, level1_inv=level1_inv, level1_panel=level1_panel, child_inv=child_inv, child_panel=child_panel, child_width=child_width, child_parent=child_parent, child_blocks=child_blocks)


highest = lax.Precision.HIGHEST


def product(former, latter):
    return jnp.dot(former, latter, precision=highest, preferred_element_type=jnp.float32)


def child_leverage(ancestor, factor, panel, width, blocks):
    columns = jnp.arange(CHILD_COLS, dtype=jnp.int32)
    live = (columns < width).astype(jnp.float32)
    normal = panel * live[None, :]
    masked = factor * live[:, None] * live[None, :]
    offsets = jnp.arange(BLOCK_ROWS, dtype=jnp.int32)
    slots = (blocks[:, None] * BLOCK_ROWS + offsets[None, :]).reshape(-1).astype(jnp.int32)
    picked = jnp.take(jnp.take(ancestor, slots, axis=0), slots, axis=1)
    image = product(picked, normal)
    return jnp.sum(masked * masked, axis=0) + jnp.sum(normal * image, axis=0)


def reference(root_inv, level1_inv, level1_panel, child_inv, child_panel, child_width, child_parent, child_blocks):
    root_cov = product(root_inv.T, root_inv)
    leverage_root = jnp.diagonal(root_cov)
    crossings = []
    parent_blocks = []
    for member in range(PARENTS):
        panel = level1_panel[:, member, :]
        factor = level1_inv[:, member, :]
        crossing = product(root_cov, panel)
        crossings.append(crossing)
        parent_blocks.append(product(factor.T, factor) + product(panel.T, crossing))
    parent_cross = jnp.stack(crossings)
    parent_cov = jnp.stack(parent_blocks)
    leverage_parent = jnp.stack([jnp.diagonal(block) for block in parent_blocks])
    results = []
    for member in range(CHILDREN):
        parent = child_parent[member]
        crossing = lax.dynamic_index_in_dim(parent_cross, parent, 0, keepdims=False)
        diagonal_block = lax.dynamic_index_in_dim(parent_cov, parent, 0, keepdims=False)
        ancestor = jnp.concatenate([
            jnp.concatenate([root_cov, -crossing], axis=1),
            jnp.concatenate([-crossing.T, diagonal_block], axis=1)], axis=0)
        results.append(child_leverage(ancestor, child_inv[member], child_panel[member], child_width[member], child_blocks[member]))
    return leverage_root, leverage_parent, jnp.stack(results)
```

```python
import jax
import jax.numpy as jnp
from jax import lax
from jax.experimental import pallas as pl
from jax.experimental.pallas import tpu as pltpu
from jax.sharding import PartitionSpec as P

BLOCK_ROWS = 32
PAIRS = [(i, i ^ 1) for i in range(32)]
SAME_CORE = [[2 * m + k for m in range(16)] for k in range(2)]
f32 = jnp.float32
bf16 = jnp.bfloat16

VMEM = pl.BlockSpec(memory_space=pltpu.VMEM)
SMEM = pl.BlockSpec(memory_space=pltpu.SMEM)
PARAMS = pltpu.CompilerParams(vmem_limit_bytes=48 * 1024 * 1024)


def call(kernel, outs, specs, flops, nbytes, scratch=()):
    return pl.pallas_call(
        kernel,
        out_shape=[jax.ShapeDtypeStruct(s, d) for s, d in outs],
        in_specs=specs,
        out_specs=[VMEM] * len(outs),
        scratch_shapes=list(scratch),
        compiler_params=PARAMS,
        cost_estimate=pl.CostEstimate(flops=flops, bytes_accessed=nbytes, transcendentals=0),
    )


def split(x):
    high = x.astype(bf16)
    return high, (x - high.astype(f32)).astype(bf16)


def dot(a, b):
    return jnp.dot(a, b, preferred_element_type=f32)


def squares(x):
    return jnp.sum(x * x, axis=0, keepdims=True)


def kids_of(parents, which):
    hit = [parents[j] == which for j in range(4)]
    first = jnp.where(hit[0], 0, jnp.where(hit[1], 1, 2))
    second = jnp.where(hit[3], 3, jnp.where(hit[2], 2, 1))
    return first, second


def pack_kernel(ids, parents, widths, panel, level1, child, keep, give):
    for out, which in ((keep, ids[0]), (give, 1 - ids[0])):
        out[0:128, :] = panel[pl.ds(which, 128, stride=2), :]
        lanes = ids[1] * 128 + lax.broadcasted_iota(jnp.int32, (64, 128), 1)
        for place, kid in enumerate(kids_of(parents, which)):
            live = lanes < widths[kid]
            out[128 + 64 * place : 192 + 64 * place, :] = jnp.where(live, child[kid], 0.0)
        out[256:288, :] = level1[pl.ds(which, 32, stride=2), :]


def cross_kernel(ids, mine, theirs, packed, cross, root):
    core = ids[0]
    total = jnp.zeros((256, 128), f32)
    for z in range(8):
        own = mine[z]
        root[4 * z : 4 * z + 4, :] = jnp.concatenate(
            [squares(own[:, 128 * h : 128 * h + 128]) for h in range(4)], axis=0
        )
        high, low = split(jnp.concatenate([own, theirs[z]], axis=0))
        panel = jnp.concatenate(
            [packed[2 * z + h // 2, (h % 2) ^ core, 0:128, :] for h in range(4)], axis=0
        )
        panel_high, panel_low = split(panel)
        both = dot(high, jnp.concatenate([panel_high, panel_low], axis=1))
        total = total + (both[:, :128] + both[:, 128:]) + dot(low, panel_high)
    cross[...] = total


def child_kernel(
    ids, parents, widths, blocks, mine, theirs, packed, child_inv,
    image, below_high, below_low, base, spread_high, spread_low,
):
    core = ids[0]
    spread_high[...] = jnp.zeros_like(spread_high)
    spread_low[...] = jnp.zeros_like(spread_low)
    for place, kid in enumerate(kids_of(parents, core)):
        for s in range(64):
            row = pl.multiple_of(blocks[kid, s] * BLOCK_ROWS, BLOCK_ROWS)
            start = 128 + 64 * place + 32 * (s % 2)
            piece = packed[s // 4, ((s // 2) % 2) ^ core, start : start + 32, :]
            high, low = split(piece)
            spread_high[pl.ds(row, 32), 128 * place : 128 * place + 128] = high
            spread_low[pl.ds(row, 32), 128 * place : 128 * place + 128] = low
    total = jnp.zeros((256, 256), f32)
    for z in range(8):
        high, low = split(jnp.concatenate([mine[z], theirs[z]], axis=0))
        up = spread_high[512 * z : 512 * z + 512, :]
        down = spread_low[512 * z : 512 * z + 512, :]
        total = total + dot(high, up) + dot(high, down) + dot(low, up)
    image[...] = total
    below_high[...] = spread_high[4096:5120, :]
    below_low[...] = spread_low[4096:5120, :]
    rows = ids[2] * 32 + lax.broadcasted_iota(jnp.int32, (32, 128), 0)
    lanes = ids[1] * 128 + lax.broadcasted_iota(jnp.int32, (32, 128), 1)
    for j in range(4):
        live = jnp.logical_and(rows < widths[j], lanes < widths[j])
        base[j : j + 1, :] = squares(jnp.where(live, child_inv[j], 0.0))


def finish_kernel(
    ids, parents, image, below_high, below_low, cross, level1, root, base, payload,
):
    core = ids[0]
    total = image[...]
    lower = jnp.zeros((64, 256), f32)
    sums = []
    for z in range(8):
        up = below_high[128 * z : 128 * z + 128, :]
        down = below_low[128 * z : 128 * z + 128, :]
        high, low = split(cross[z])
        total = total - (dot(high, up) + dot(high, down) + dot(low, up))
        factor = level1[z]
        high, low = split(factor)
        lower = lower + dot(high, up) + dot(high, down) + dot(low, up)
        sums.append(squares(cross[z]) + squares(factor))
    child = squares(total) + squares(lower)
    first, second = kids_of(parents, core)
    place = lax.broadcasted_iota(jnp.int32, (4, 128), 0)
    ends = (
        base[...]
        + jnp.where(place == first, child[:, :128], 0.0)
        + jnp.where(place == second, child[:, 128:], 0.0)
    )
    for i in range(32):
        line = sums[i // 4]
        payload[i, 0:4, :] = ends
        payload[i, 4:5, :] = root[i : i + 1, :]
        payload[i, 5:6, :] = jnp.where(core == 0, line, 0.0)
        payload[i, 6:7, :] = jnp.where(core == 0, 0.0, line)
        payload[i, 7:8, :] = jnp.zeros((1, 128), f32)


def body(
    root_inv,
    level1_inv,
    level1_panel,
    child_inv,
    child_panel,
    child_width,
    child_parent,
    child_blocks,
):
    row = lax.axis_index("row")
    col = lax.axis_index("col")
    ids = jnp.stack([row % 2, col, row]).astype(jnp.int32)

    mine = lax.all_gather(root_inv, "col")
    keep, give = call(
        pack_kernel, [((288, 128), f32)] * 2, [SMEM] * 3 + [VMEM] * 3, 0, 600000
    )(
        ids, child_parent, child_width,
        level1_panel.reshape(256, 128), level1_inv.reshape(64, 128), child_panel,
    )
    got = lax.ppermute(give, "row", PAIRS)
    pair = jnp.stack([keep, got])
    packed = lax.all_gather(pair[:, :256], "row", axis_index_groups=SAME_CORE)
    level1 = lax.all_gather(pair[:, 256:].reshape(64, 128), "col")
    theirs = lax.ppermute(mine, "row", PAIRS)

    cross_part, root = call(
        cross_kernel, [((256, 128), f32), ((32, 128), f32)], [SMEM] + [VMEM] * 3,
        800_000_000, 8_000_000,
    )(ids, mine, theirs, packed)
    cross = lax.all_gather(cross_part, "col")

    image, below_high, below_low, base = call(
        child_kernel,
        [((256, 256), f32), ((1024, 256), bf16), ((1024, 256), bf16), ((4, 128), f32)],
        [SMEM] * 4 + [VMEM] * 4, 1_600_000_000, 10_000_000,
        [pltpu.VMEM((5120, 256), bf16), pltpu.VMEM((5120, 256), bf16)],
    )(ids, child_parent, child_width, child_blocks, mine, theirs, packed, child_inv)

    (payload,) = call(
        finish_kernel, [((32, 8, 128), f32)], [SMEM] * 2 + [VMEM] * 7,
        500_000_000, 3_000_000,
    )(ids, child_parent, image, below_high, below_low, cross, level1, root, base)
    total = jnp.sum(lax.all_to_all(payload, "row", 0, 0, tiled=True), axis=0)
    parent = lax.dynamic_slice(total[5:7], (0, 32 * (row % 4)), (2, 32))
    return total[4], parent, total[0:4]


def solution(mesh):
    placed = (
        P("row", "col"),
        P("row", None, "col"),
        P("row", None, "col"),
        P(None, "row", "col"),
        P(None, "row", "col"),
        P(),
        P(),
        P(),
    )
    return jax.shard_map(
        body,
        mesh=mesh,
        in_specs=placed,
        out_specs=(P("row"), P(None, "row"), P(None, "col")),
        check_vma=False,
    )
```

```python
import jax
import jax.numpy as jnp
from jax import lax
from jax.experimental import pallas as pl
from jax.experimental.pallas import tpu as pltpu
from jax.sharding import PartitionSpec as P

BLOCK_ROWS = 32
PAIRS = [(i, i ^ 1) for i in range(32)]
f32 = jnp.float32
bf16 = jnp.bfloat16

VMEM = pl.BlockSpec(memory_space=pltpu.VMEM)
ANY = pl.BlockSpec(memory_space=pl.ANY)
HBM = pl.BlockSpec(memory_space=pltpu.HBM)
SMEM = pl.BlockSpec(memory_space=pltpu.SMEM)


def call(kernel, outs, ins, cost, scratch=(), mib=60):
    return pl.pallas_call(
        kernel,
        out_shape=[jax.ShapeDtypeStruct(*out) for out in outs],
        in_specs=ins,
        out_specs=[VMEM] * len(outs),
        scratch_shapes=list(scratch),
        compiler_params=pltpu.CompilerParams(vmem_limit_bytes=60 * 1024 * 1024),
        cost_estimate=pl.CostEstimate(flops=cost[0], bytes_accessed=cost[1], transcendentals=0),
    )


def split(x):
    high = x.astype(bf16)
    return high, (x - high.astype(f32)).astype(bf16)


def dot(a, b):
    return jnp.dot(a, b, preferred_element_type=f32)


def product(x, high, low):
    up, down = split(x)
    rows = x.shape[0]
    both = dot(jnp.concatenate([up, down], axis=0), high)
    return both[:rows] + both[rows:] + dot(up, low)


def squares(x):
    return jnp.sum(x * x, axis=0, keepdims=True)


def kids_in_order(parents):
    order = []
    for which in range(2):
        hit = [parents[j] == which for j in range(4)]
        order.append(jnp.where(hit[0], 0, jnp.where(hit[1], 1, 2)))
        order.append(jnp.where(hit[3], 3, jnp.where(hit[2], 2, 1)))
    return order


def pack_kernel(root_inv, level1, panel, out, apart):
    out[0:128, :] = root_inv[...]
    for which in range(2):
        apart[which] = panel[pl.ds(which, 128, stride=2), :]
    for q in range(4):
        out[128:144, 128 * q : 128 * q + 128] = level1[16 * q : 16 * q + 16, :]


def chip_of(ids):
    return ids[2] // 8, (ids[2] // 2) % 4


def fetch_plane(parts, into, arrived):
    copies = []
    for side in range(2):
        zero, one, three, low, high = parts[5 * side : 5 * side + 5]
        for part, far, steps in (
            (zero, 0, (0, 1, 2, 3)),
            (one, 1, (0, 1, 2, 3)),
            (three, 3, (0, 1, 2, 3)),
            (low, 2, (0, 1)),
            (high, 2, (2, 3)),
        ):
            spot = into.at[4 * side + far, pl.ds(steps[0], len(steps))]
            copy = pltpu.make_async_copy(part, spot, arrived.at[len(copies)])
            copies.append((copy, side, far, steps))
    return copies


def fetch_rows(rows, factor, arrived):
    return [
        pltpu.make_async_copy(rows.at[z, pl.ds(0, 128)], factor.at[z], arrived.at[z])
        for z in range(8)
    ]


def split_rows(copies, factor, both):
    for z, copy in enumerate(copies):
        copy.wait()
        high, low = split(factor[z])
        both[0:128, 512 * z : 512 * z + 512] = high
        both[128:256, 512 * z : 512 * z + 512] = low


def times_rows(both, high, low):
    first = dot(both[...], high)
    return first[:128] + first[128:] + dot(both[0:128, :], low)


def cross_kernel(ids, rows, *refs):
    parts, refs = refs[:10], refs[10:]
    cross, root, factor, panels, both, high, low, row_here, panel_here = refs
    row_copies = fetch_rows(rows, factor, row_here)
    copies = fetch_plane(parts, panels, panel_here)
    for copy in row_copies + [c[0] for c in copies]:
        copy.start()
    split_rows(row_copies, factor, both)
    for z in range(8):
        root[z] = squares(factor[z])
    chip_y, chip_x = chip_of(ids)
    for copy, side, far, steps in copies:
        copy.wait()
        core = ids[0] if side == 0 else 1 - ids[0]
        for step in steps:
            chip = (chip_y + 4 - step) % 4 * 4 + (chip_x + 4 - far) % 4
            spot = pl.ds(pl.multiple_of(128 * (2 * chip + core), 128), 128)
            for which in range(2):
                up, down = split(panels[4 * side + far, step, which])
                high[spot, 128 * which : 128 * which + 128] = up
                low[spot, 128 * which : 128 * which + 128] = down
    cross[...] = times_rows(both, high[...], low[...])


def child_kernel(ids, parents, widths, blocks, rows, child_inv, *refs):
    parts, refs = refs[:10], refs[10:]
    image, below_high, below_low, base, lines = refs[:5]
    factor, level1, panels, both, high, low, row_here, part_here, tail_here = refs[5:]
    copies = fetch_plane(parts, panels, part_here)
    row_copies = fetch_rows(rows, factor, row_here)
    tail = pltpu.make_async_copy(rows.at[:, pl.ds(128, 16)], level1, tail_here)
    for copy in [c[0] for c in copies] + row_copies + [tail]:
        copy.start()
    high[...] = jnp.zeros_like(high)
    low[...] = jnp.zeros_like(low)
    chip_y, chip_x = chip_of(ids)
    lanes = ids[1] * 128 + lax.broadcasted_iota(jnp.int32, (32, 128), 1)
    order = kids_in_order(parents)
    live = [lanes < widths[kid] for kid in order]
    for copy, side, far, steps in copies:
        copy.wait()
        core = ids[0] if side == 0 else 1 - ids[0]
        for step in steps:
            chip = (chip_y + 4 - far) % 4 * 4 + (chip_x + 4 - step) % 4
            for half in range(2):
                slot = 4 * chip + 2 * core + half
                for place, kid in enumerate(order):
                    row = pl.multiple_of(blocks[kid, slot] * BLOCK_ROWS, BLOCK_ROWS)
                    piece = panels[4 * side + far, step, kid, 32 * half : 32 * half + 32, :]
                    up, down = split(jnp.where(live[place], piece, 0.0))
                    high[pl.ds(row, 32), 128 * place : 128 * place + 128] = up
                    low[pl.ds(row, 32), 128 * place : 128 * place + 128] = down
    split_rows(row_copies, factor, both)
    image[...] = times_rows(both, high[0:4096, :], low[0:4096, :])
    below_high[...] = high[4096:5120, :]
    below_low[...] = low[4096:5120, :]

    depth = ids[2] * 32 + lax.broadcasted_iota(jnp.int32, (32, 128), 0)
    for j in range(4):
        inside = jnp.logical_and(depth < widths[j], lanes < widths[j])
        base[j : j + 1, :] = squares(jnp.where(inside, child_inv[j], 0.0))
    tail.wait()
    own = jnp.concatenate(
        [
            jnp.concatenate([level1[n, :, 128 * q : 128 * q + 128] for n in range(8)], axis=1)
            for q in range(4)
        ],
        axis=0,
    )
    lower = product(own, high[4096:5120, :], low[4096:5120, :])
    parity = lax.broadcasted_iota(jnp.int32, (64, 1024), 0) % 2
    parity_half = lax.broadcasted_iota(jnp.int32, (64, 256), 0) % 2
    for which in range(2):
        half = slice(256 * which, 256 * which + 256)
        sums = squares(jnp.where(parity_half == which, lower[:, half], 0.0))
        base[...] += by_child(parents, which, sums)
        lines[which : which + 1, :] = squares(jnp.where(parity == which, own, 0.0))


def by_child(parents, which, sums):
    place = lax.broadcasted_iota(jnp.int32, (4, 128), 0)
    first, second = kids_in_order(parents)[2 * which : 2 * which + 2]
    return jnp.where(place == first, sums[:, :128], 0.0) + jnp.where(
        place == second, sums[:, 128:], 0.0
    )


def finish_kernel(ids, parents, root, base, lines, image, below_high, below_low, *refs):
    parts, (payload, cross, arrived) = refs[:9], refs[9:]
    copies = []
    for n, part in enumerate(parts):
        away = (0, 1, -1, 2, -2, 3, -3, 4, 4)[n]
        spot = cross.at[(ids[1] + 8 - away) % 8]
        if n >= 7:
            spot = spot.at[pl.ds(64 * (n - 7), 64)]
        copies.append(pltpu.make_async_copy(part, spot, arrived.at[n]))
    for copy in copies:
        copy.start()
    for copy in copies:
        copy.wait()
    ends = base[...]
    known_lines = []
    for which in range(2):
        half = slice(256 * which, 256 * which + 256)
        known = jnp.concatenate(
            [cross[z, :, 128 * which : 128 * which + 128] for z in range(8)], axis=1
        )
        upper = image[:, half] - product(known, below_high[:, half], below_low[:, half])
        ends = ends + by_child(parents, which, squares(upper))
        known_lines.append(lines[which : which + 1, :] + squares(known))
    for i in range(32):
        b = i // 4
        payload[i, 0:4, :] = ends
        payload[i, 4:5, :] = root[b, :, 128 * (i % 4) : 128 * (i % 4) + 128]
        payload[i, 5:6, :] = known_lines[0][:, 128 * b : 128 * b + 128]
        payload[i, 6:7, :] = known_lines[1][:, 128 * b : 128 * b + 128]
        payload[i, 7:8, :] = jnp.zeros((1, 128), f32)


def sum_kernel(ids, parts, root, parent, child):
    total = parts[0]
    for i in range(1, 32):
        total = total + parts[i]
    child[...] = total[0:4, :]
    root[...] = total[4:5, :]
    place = ids[2] % 4
    found = total[5:7, 0:32]
    for n in range(1, 4):
        found = jnp.where(place == n, total[5:7, 32 * n : 32 * n + 32], found)
    parent[...] = found


def moved(x, down, right):
    def target(i):
        y, x, core = i // 8, i // 2 % 4, i % 2
        return ((y + down) % 4 * 4 + (x + right) % 4) * 2 + core

    return lax.ppermute(x, "row", [(i, target(i)) for i in range(32)])


def around(x, step):
    one, three = step(x, 1), step(x, 3)
    return [x, one, three, step(one[:2], 1), step(three[2:], 3)]


def along(x, meanwhile):
    def moved(part, n):
        return lax.ppermute(part, "col", [(z, (z + n) % 8) for z in range(8)])

    first, meanwhile = lax.optimization_barrier(
        ([moved(x, n) for n in (1, -1, 2, -2)], meanwhile)
    )
    below, above = first[2:]
    second = [moved(below, 1), moved(above, -1), moved(below[:64], 2), moved(above[64:], -2)]
    return [x] + first + second, meanwhile


def body(
    root_inv,
    level1_inv,
    level1_panel,
    child_inv,
    child_panel,
    child_width,
    child_parent,
    child_blocks,
):
    row = lax.axis_index("row")
    col = lax.axis_index("col")
    ids = jnp.stack([row & 1, col, row]).astype(jnp.int32)

    packed, panel = call(
        pack_kernel, [((144, 512), f32), ((2, 128, 128), f32)], [VMEM] * 3, (0, 900_000)
    )(root_inv, level1_inv.reshape(64, 128), level1_panel.reshape(256, 128))
    rows = lax.all_gather(packed, "col")

    panels = jnp.stack([panel] + [moved(panel, n, 0) for n in (1, 2, 3)])
    children = jnp.stack([child_panel] + [moved(child_panel, 0, n) for n in (1, 2, 3)])
    panels = around(panels, lambda x, n: moved(x, 0, n))
    children = around(children, lambda x, n: moved(x, n, 0))
    panels = panels + [lax.ppermute(part, "row", PAIRS) for part in panels]
    panels, children = lax.optimization_barrier((panels, children))
    children = children + [lax.ppermute(part, "row", PAIRS) for part in children]

    cross, root = call(
        cross_kernel, [((128, 256), f32), ((8, 1, 512), f32)],
        [SMEM] + [HBM] * 11, (800_000_000, 6_000_000),
        [
            pltpu.VMEM((8, 128, 512), f32),
            pltpu.VMEM((8, 4, 2, 128, 128), f32),
            pltpu.VMEM((256, 4096), bf16),
            pltpu.VMEM((4096, 256), bf16),
            pltpu.VMEM((4096, 256), bf16),
            pltpu.SemaphoreType.DMA((8,)),
            pltpu.SemaphoreType.DMA((10,)),
        ],
    )(ids, rows, *panels)
    cross, children = lax.optimization_barrier((cross, children))

    worked = call(
        child_kernel,
        [
            ((128, 512), f32), ((1024, 512), bf16), ((1024, 512), bf16),
            ((4, 128), f32), ((2, 1024), f32),
        ],
        [SMEM] * 4 + [HBM, VMEM] + [HBM] * 10, (1_600_000_000, 10_000_000),
        [
            pltpu.VMEM((8, 128, 512), f32),
            pltpu.VMEM((8, 16, 512), f32),
            pltpu.VMEM((8, 4, 4, 64, 128), f32),
            pltpu.VMEM((256, 4096), bf16),
            pltpu.VMEM((5120, 512), bf16),
            pltpu.VMEM((5120, 512), bf16),
            pltpu.SemaphoreType.DMA((8,)),
            pltpu.SemaphoreType.DMA((10,)),
            pltpu.SemaphoreType.DMA,
        ],
        40,
    )(ids, child_parent, child_width, child_blocks, rows, child_inv, *children)
    crosses, (image, below_high, below_low, base, lines) = along(cross, worked)

    (payload,) = call(
        finish_kernel, [((32, 8, 128), f32)], [SMEM] * 2 + [VMEM] * 6 + [ANY] * 9,
        (500_000_000, 3_000_000),
        [pltpu.VMEM((8, 128, 256), f32), pltpu.SemaphoreType.DMA((9,))],
        16,
    )(ids, child_parent, root, base, lines, image, below_high, below_low, *crosses)
    root, parent, child = call(
        sum_kernel, [((1, 128), f32), ((2, 32), f32), ((4, 128), f32)], [SMEM, VMEM],
        (0, 130_000), (), 16,
    )(ids, lax.all_to_all(payload, "row", 0, 0, tiled=True))
    return root.reshape(128), parent, child


def solution(mesh):
    placed = (
        P("row", "col"),
        P("row", None, "col"),
        P("row", None, "col"),
        P(None, "row", "col"),
        P(None, "row", "col"),
        P(),
        P(),
        P(),
    )
    return jax.shard_map(
        body,
        mesh=mesh,
        in_specs=placed,
        out_specs=(P("row"), P(None, "row"), P(None, "col")),
        check_vma=False,
    )
```

```python
import jax
import jax.numpy as jnp
from jax import lax
from jax.experimental import pallas as pl
from jax.experimental.pallas import tpu as pltpu
from jax.sharding import PartitionSpec as P

BLOCK_ROWS = 32
PAIRS = [(i, i ^ 1) for i in range(32)]
SAME_CORE = [[2 * m + k for m in range(16)] for k in range(2)]
f32 = jnp.float32
bf16 = jnp.bfloat16

VMEM = pl.BlockSpec(memory_space=pltpu.VMEM)
ANY = pl.BlockSpec(memory_space=pl.ANY)
HBM = pl.BlockSpec(memory_space=pltpu.HBM)
SMEM = pl.BlockSpec(memory_space=pltpu.SMEM)


def call(kernel, outs, ins, cost, scratch=(), mib=60):
    return pl.pallas_call(
        kernel,
        out_shape=[jax.ShapeDtypeStruct(*out) for out in outs],
        in_specs=ins,
        out_specs=[VMEM] * len(outs),
        scratch_shapes=list(scratch),
        compiler_params=pltpu.CompilerParams(vmem_limit_bytes=60 * 1024 * 1024),
        cost_estimate=pl.CostEstimate(flops=cost[0], bytes_accessed=cost[1], transcendentals=0),
    )


def split(x):
    high = x.astype(bf16)
    return high, (x - high.astype(f32)).astype(bf16)


def dot(a, b):
    return jnp.dot(a, b, preferred_element_type=f32)


def product(x, high, low):
    up, down = split(x)
    rows = x.shape[0]
    both = dot(jnp.concatenate([up, down], axis=0), high)
    return both[:rows] + both[rows:] + dot(up, low)


def squares(x):
    return jnp.sum(x * x, axis=0, keepdims=True)


def kids_in_order(parents):
    order = []
    for which in range(2):
        hit = [parents[j] == which for j in range(4)]
        order.append(jnp.where(hit[0], 0, jnp.where(hit[1], 1, 2)))
        order.append(jnp.where(hit[3], 3, jnp.where(hit[2], 2, 1)))
    return order


def pack_kernel(root_inv, level1, panel, child, out, panels, children):
    out[0:128, :] = root_inv[...]
    for which in range(2):
        apart = panel[pl.ds(which, 128, stride=2), :]
        for n in range(16):
            panels[n, which] = apart
    whole = child[...]
    for n in range(16):
        children[n] = whole
    for q in range(4):
        out[128:144, 128 * q : 128 * q + 128] = level1[16 * q : 16 * q + 16, :]


def chip_of(ids):
    return ids[2] // 8, (ids[2] // 2) % 4


def fetch_rows(ids, parts, factor, tail, arrived):
    copies = []
    for n, away in enumerate((0, 1, 2, 3, 4, 7, 6, 5)):
        z = (ids[1] + 8 - away) % 8
        copies.append(
            pltpu.make_async_copy(parts[n].at[pl.ds(0, 128)], factor.at[z], arrived.at[n])
        )
        if tail is not None:
            copies.append(
                pltpu.make_async_copy(
                    parts[n].at[pl.ds(128, 16)], tail.at[z], arrived.at[8 + n]
                )
            )
    return copies


def split_rows(copies, factor, both):
    for copy in copies:
        copy.wait()
    for z in range(8):
        high, low = split(factor[z])
        both[0:128, 512 * z : 512 * z + 512] = high
        both[128:256, 512 * z : 512 * z + 512] = low


def times_rows(both, high, low):
    first = dot(both[...], high)
    return first[:128] + first[128:] + dot(both[0:128, :], low)


def cross_kernel(ids, *refs):
    parts, sides, refs = refs[:8], refs[8:10], refs[10:]
    cross, root, factor, panels, both, high, low, row_here, panel_here = refs
    row_copies = fetch_rows(ids, parts, factor, None, row_here)
    copies = [
        pltpu.make_async_copy(side, panels.at[n], panel_here.at[n])
        for n, side in enumerate(sides)
    ]
    for copy in copies + row_copies:
        copy.start()
    for n, copy in enumerate(copies):
        copy.wait()
        core = ids[0] if n == 0 else 1 - ids[0]
        for chip in range(16):
            spot = pl.ds(pl.multiple_of(128 * (2 * chip + core), 128), 128)
            for which in range(2):
                up, down = split(panels[n, chip, which])
                high[spot, 128 * which : 128 * which + 128] = up
                low[spot, 128 * which : 128 * which + 128] = down
    split_rows(row_copies, factor, both)
    for z in range(8):
        root[z] = squares(factor[z])
    cross[...] = times_rows(both, high[...], low[...])


def child_kernel(ids, parents, widths, blocks, child_inv, *refs):
    rows, sides, refs = refs[:8], refs[8:10], refs[10:]
    image, below_high, below_low, base, lines = refs[:5]
    factor, level1, panels, both, high, low, row_here, part_here = refs[5:]
    copies = [
        pltpu.make_async_copy(side, panels.at[n], part_here.at[n])
        for n, side in enumerate(sides)
    ]
    row_copies = fetch_rows(ids, rows, factor, level1, row_here)
    for copy in copies + row_copies:
        copy.start()
    high[...] = jnp.zeros_like(high)
    low[...] = jnp.zeros_like(low)
    lanes = ids[1] * 128 + lax.broadcasted_iota(jnp.int32, (32, 128), 1)
    order = kids_in_order(parents)
    live = [lanes < widths[kid] for kid in order]
    for n, copy in enumerate(copies):
        copy.wait()
        core = ids[0] if n == 0 else 1 - ids[0]
        for chip in range(16):
            for half in range(2):
                slot = 4 * chip + 2 * core + half
                for place, kid in enumerate(order):
                    row = pl.multiple_of(blocks[kid, slot] * BLOCK_ROWS, BLOCK_ROWS)
                    piece = panels[n, chip, kid, 32 * half : 32 * half + 32, :]
                    up, down = split(jnp.where(live[place], piece, 0.0))
                    high[pl.ds(row, 32), 128 * place : 128 * place + 128] = up
                    low[pl.ds(row, 32), 128 * place : 128 * place + 128] = down
    split_rows(row_copies, factor, both)
    image[...] = times_rows(both, high[0:4096, :], low[0:4096, :])
    below_high[...] = high[4096:5120, :]
    below_low[...] = low[4096:5120, :]

    depth = ids[2] * 32 + lax.broadcasted_iota(jnp.int32, (32, 128), 0)
    for j in range(4):
        inside = jnp.logical_and(depth < widths[j], lanes < widths[j])
        base[j : j + 1, :] = squares(jnp.where(inside, child_inv[j], 0.0))
    own = jnp.concatenate(
        [
            jnp.concatenate([level1[n, :, 128 * q : 128 * q + 128] for n in range(8)], axis=1)
            for q in range(4)
        ],
        axis=0,
    )
    lower = product(own, high[4096:5120, :], low[4096:5120, :])
    parity = lax.broadcasted_iota(jnp.int32, (64, 1024), 0) % 2
    parity_half = lax.broadcasted_iota(jnp.int32, (64, 256), 0) % 2
    for which in range(2):
        half = slice(256 * which, 256 * which + 256)
        sums = squares(jnp.where(parity_half == which, lower[:, half], 0.0))
        base[...] += by_child(parents, which, sums)
        lines[which : which + 1, :] = squares(jnp.where(parity == which, own, 0.0))


def by_child(parents, which, sums):
    place = lax.broadcasted_iota(jnp.int32, (4, 128), 0)
    first, second = kids_in_order(parents)[2 * which : 2 * which + 2]
    return jnp.where(place == first, sums[:, :128], 0.0) + jnp.where(
        place == second, sums[:, 128:], 0.0
    )


def finish_kernel(ids, parents, root, base, lines, image, below_high, below_low, *refs):
    parts, (payload, cross, arrived) = refs[:8], refs[8:]
    copies = []
    for n, away in enumerate((0, 1, 7, 2, 6, 4, 3, 5)):
        spot = cross.at[(ids[1] + 8 - away) % 8]
        copies.append(pltpu.make_async_copy(parts[n], spot, arrived.at[n]))
    for copy in copies:
        copy.start()
    for copy in copies:
        copy.wait()
    ends = base[...]
    known_lines = []
    for which in range(2):
        half = slice(256 * which, 256 * which + 256)
        known = jnp.concatenate(
            [cross[z, :, 128 * which : 128 * which + 128] for z in range(8)], axis=1
        )
        upper = image[:, half] - product(known, below_high[:, half], below_low[:, half])
        ends = ends + by_child(parents, which, squares(upper))
        known_lines.append(lines[which : which + 1, :] + squares(known))
    for i in range(32):
        b = i // 4
        payload[i, 0:4, :] = ends
        payload[i, 4:5, :] = root[b, :, 128 * (i % 4) : 128 * (i % 4) + 128]
        payload[i, 5:6, :] = known_lines[0][:, 128 * b : 128 * b + 128]
        payload[i, 6:7, :] = known_lines[1][:, 128 * b : 128 * b + 128]
        payload[i, 7:8, :] = jnp.zeros((1, 128), f32)


def sum_kernel(ids, parts, root, parent, child):
    total = parts[0]
    for i in range(1, 32):
        total = total + parts[i]
    child[...] = total[0:4, :]
    root[...] = total[4:5, :]
    place = ids[2] % 4
    found = total[5:7, 0:32]
    for n in range(1, 4):
        found = jnp.where(place == n, total[5:7, 32 * n : 32 * n + 32], found)
    parent[...] = found


def moved(x, down, right):
    def target(i):
        y, x, core = i // 8, i // 2 % 4, i % 2
        return ((y + down) % 4 * 4 + (x + right) % 4) * 2 + core

    return lax.ppermute(x, "row", [(i, target(i)) for i in range(32)])


def along(x, n):
    return lax.ppermute(x, "col", [(z, (z + n) % 8) for z in range(8)])


def body(
    root_inv,
    level1_inv,
    level1_panel,
    child_inv,
    child_panel,
    child_width,
    child_parent,
    child_blocks,
):
    row = lax.axis_index("row")
    col = lax.axis_index("col")
    ids = jnp.stack([row & 1, col, row]).astype(jnp.int32)

    packed, panels, children = call(
        pack_kernel,
        [((144, 512), f32), ((16, 2, 128, 128), f32), ((16, 4, 64, 128), f32)],
        [VMEM] * 4, (0, 5_000_000),
    )(root_inv, level1_inv.reshape(64, 128), level1_panel.reshape(256, 128), child_panel)
    fence = lax.optimization_barrier
    down, up = [packed], [packed]
    for n in range(3):
        down.append(along(down[-1], 1))
        up.append(along(up[-1], -1))
    mine = lax.all_to_all(
        panels, "row", 0, 0, tiled=True, axis_index_groups=SAME_CORE
    )
    mine, children, down[3], up[3] = fence((mine, children, down[3], up[3]))
    rows = down + [along(down[3], 1)] + up[1:]
    panels = [mine, lax.ppermute(mine, "row", PAIRS)]
    mine = lax.all_to_all(
        children, "row", 0, 0, tiled=True, axis_index_groups=SAME_CORE
    )

    cross, root = call(
        cross_kernel, [((128, 256), f32), ((8, 1, 512), f32)],
        [SMEM] + [HBM] * 8 + [ANY, HBM], (40_000_000_000, 6_000_000),
        [
            pltpu.VMEM((8, 128, 512), f32),
            pltpu.VMEM((2, 16, 2, 128, 128), f32),
            pltpu.VMEM((256, 4096), bf16),
            pltpu.VMEM((4096, 256), bf16),
            pltpu.VMEM((4096, 256), bf16),
            pltpu.SemaphoreType.DMA((8,)),
            pltpu.SemaphoreType.DMA((2,)),
        ],
        32,
    )(ids, *rows, *panels)
    crosses = [along(cross, n) for n in (1, -1, 2, -2, 4)]
    crosses = [cross] + crosses + [along(crosses[2], 1), along(crosses[3], -1)]
    mine, _ = fence((mine, crosses))
    children = [mine, lax.ppermute(mine, "row", PAIRS)]

    image, below_high, below_low, base, lines = call(
        child_kernel,
        [
            ((128, 512), f32), ((1024, 512), bf16), ((1024, 512), bf16),
            ((4, 128), f32), ((2, 1024), f32),
        ],
        [SMEM] * 4 + [VMEM] + [HBM] * 8 + [ANY, HBM], (1_600_000_000, 10_000_000),
        [
            pltpu.VMEM((8, 128, 512), f32),
            pltpu.VMEM((8, 16, 512), f32),
            pltpu.VMEM((2, 16, 4, 64, 128), f32),
            pltpu.VMEM((256, 4096), bf16),
            pltpu.VMEM((5120, 512), bf16),
            pltpu.VMEM((5120, 512), bf16),
            pltpu.SemaphoreType.DMA((16,)),
            pltpu.SemaphoreType.DMA((2,)),
        ],
        30,
    )(ids, child_parent, child_width, child_blocks, child_inv, *rows, *children)

    (payload,) = call(
        finish_kernel, [((32, 8, 128), f32)], [SMEM] * 2 + [VMEM] * 6 + [ANY] * 8,
        (500_000_000, 3_000_000),
        [pltpu.VMEM((8, 128, 256), f32), pltpu.SemaphoreType.DMA((8,))],
        16,
    )(ids, child_parent, root, base, lines, image, below_high, below_low, *crosses)
    root, parent, child = call(
        sum_kernel, [((1, 128), f32), ((2, 32), f32), ((4, 128), f32)], [SMEM, VMEM],
        (0, 130_000), (), 16,
    )(ids, lax.all_to_all(payload, "row", 0, 0, tiled=True))
    return root.reshape(128), parent, child


def solution(mesh):
    placed = (
        P("row", "col"),
        P("row", None, "col"),
        P("row", None, "col"),
        P(None, "row", "col"),
        P(None, "row", "col"),
        P(),
        P(),
        P(),
    )
    return jax.shard_map(
        body,
        mesh=mesh,
        in_specs=placed,
        out_specs=(P("row"), P(None, "row"), P(None, "col")),
        check_vma=False,
    )
```

```python
import jax
import jax.numpy as jnp
from jax import lax
from jax.experimental import pallas as pl
from jax.experimental.pallas import tpu as pltpu
from jax.sharding import PartitionSpec as P

BLOCK_ROWS = 32
PAIRS = [(i, i ^ 1) for i in range(32)]
SAME_CORE = [[2 * m + k for m in range(16)] for k in range(2)]
f32 = jnp.float32
bf16 = jnp.bfloat16

VMEM = pl.BlockSpec(memory_space=pltpu.VMEM)
ANY = pl.BlockSpec(memory_space=pl.ANY)
HBM = pl.BlockSpec(memory_space=pltpu.HBM)
SMEM = pl.BlockSpec(memory_space=pltpu.SMEM)


def call(kernel, outs, ins, cost, scratch=(), mib=60):
    return pl.pallas_call(
        kernel,
        out_shape=[jax.ShapeDtypeStruct(*out) for out in outs],
        in_specs=ins,
        out_specs=[VMEM] * len(outs),
        scratch_shapes=list(scratch),
        compiler_params=pltpu.CompilerParams(vmem_limit_bytes=60 * 1024 * 1024),
        cost_estimate=pl.CostEstimate(flops=cost[0], bytes_accessed=cost[1], transcendentals=0),
    )


def split(x):
    high = x.astype(bf16)
    return high, (x - high.astype(f32)).astype(bf16)


def dot(a, b):
    return jnp.dot(a, b, preferred_element_type=f32)


def product(x, high, low):
    up, down = split(x)
    rows = x.shape[0]
    both = dot(jnp.concatenate([up, down], axis=0), high)
    return both[:rows] + both[rows:] + dot(up, low)


def squares(x):
    return jnp.sum(x * x, axis=0, keepdims=True)


def kids_in_order(parents):
    order = []
    for which in range(2):
        hit = [parents[j] == which for j in range(4)]
        order.append(jnp.where(hit[0], 0, jnp.where(hit[1], 1, 2)))
        order.append(jnp.where(hit[3], 3, jnp.where(hit[2], 2, 1)))
    return order


def pack_kernel(root_inv, level1, panel, child, out, panels, children):
    out[0:128, :] = root_inv[...]
    for which in range(2):
        apart = panel[pl.ds(which, 128, stride=2), :]
        for n in range(16):
            panels[n, which] = apart
    whole = child[...]
    for n in range(16):
        children[n] = whole
    for q in range(4):
        out[128:144, 128 * q : 128 * q + 128] = level1[16 * q : 16 * q + 16, :]


def chip_of(ids):
    return ids[2] // 8, (ids[2] // 2) % 4


def fetch_rows(ids, parts, factor, tail, arrived):
    copies = []
    for n, away in enumerate((0, 1, 2, 3, 4, 7, 6, 5)):
        z = (ids[1] + 8 - away) % 8
        copies.append(
            pltpu.make_async_copy(parts[n].at[pl.ds(0, 128)], factor.at[z], arrived.at[n])
        )
        if tail is not None:
            copies.append(
                pltpu.make_async_copy(
                    parts[n].at[pl.ds(128, 16)], tail.at[z], arrived.at[8 + n]
                )
            )
    return copies


def split_rows(copies, factor, both):
    for copy in copies:
        copy.wait()
    for z in range(8):
        high, low = split(factor[z])
        both[0:128, 512 * z : 512 * z + 512] = high
        both[128:256, 512 * z : 512 * z + 512] = low


def times_rows(both, high, low):
    first = dot(both[...], high)
    return first[:128] + first[128:] + dot(both[0:128, :], low)


def cross_kernel(ids, *refs):
    parts, sides, refs = refs[:8], refs[8:10], refs[10:]
    cross, root, factor, panels, both, high, low, row_here, panel_here = refs
    row_copies = fetch_rows(ids, parts, factor, None, row_here)
    copies = [
        pltpu.make_async_copy(side, panels.at[n], panel_here.at[n])
        for n, side in enumerate(sides)
    ]
    for copy in copies + row_copies:
        copy.start()
    for n, copy in enumerate(copies):
        copy.wait()
        core = ids[0] if n == 0 else 1 - ids[0]
        for chip in range(16):
            spot = pl.ds(pl.multiple_of(128 * (2 * chip + core), 128), 128)
            for which in range(2):
                up, down = split(panels[n, chip, which])
                high[spot, 128 * which : 128 * which + 128] = up
                low[spot, 128 * which : 128 * which + 128] = down
    split_rows(row_copies, factor, both)
    for z in range(8):
        root[z] = squares(factor[z])
    cross[...] = times_rows(both, high[...], low[...])


def child_kernel(ids, parents, widths, blocks, child_inv, root, *refs):
    rows, sides, parts, refs = refs[:8], refs[8:10], refs[10:18], refs[18:]
    payload, factor, level1, panels, cross, both, high, low = refs[:8]
    row_here, part_here, cross_here = refs[8:]
    cross_copies = [
        pltpu.make_async_copy(
            parts[n], cross.at[(ids[1] + 8 - away) % 8], cross_here.at[n]
        )
        for n, away in enumerate((0, 1, 7, 2, 6, 4, 3, 5))
    ]
    copies = [
        pltpu.make_async_copy(side, panels.at[n], part_here.at[n])
        for n, side in enumerate(sides)
    ]
    row_copies = fetch_rows(ids, rows, factor, level1, row_here)
    for copy in copies + row_copies + cross_copies:
        copy.start()
    high[...] = jnp.zeros_like(high)
    low[...] = jnp.zeros_like(low)
    lanes = ids[1] * 128 + lax.broadcasted_iota(jnp.int32, (32, 128), 1)
    order = kids_in_order(parents)
    live = [lanes < widths[kid] for kid in order]
    for n, copy in enumerate(copies):
        copy.wait()
        core = ids[0] if n == 0 else 1 - ids[0]
        for chip in range(16):
            for half in range(2):
                slot = 4 * chip + 2 * core + half
                for place, kid in enumerate(order):
                    row = pl.multiple_of(blocks[kid, slot] * BLOCK_ROWS, BLOCK_ROWS)
                    piece = panels[n, chip, kid, 32 * half : 32 * half + 32, :]
                    up, down = split(jnp.where(live[place], piece, 0.0))
                    high[pl.ds(row, 32), 128 * place : 128 * place + 128] = up
                    low[pl.ds(row, 32), 128 * place : 128 * place + 128] = down
    split_rows(row_copies, factor, both)
    image = times_rows(both, high[0:4096, :], low[0:4096, :])
    below_high, below_low = high[4096:5120, :], low[4096:5120, :]
    depth = ids[2] * 32 + lax.broadcasted_iota(jnp.int32, (32, 128), 0)
    ends = []
    for j in range(4):
        inside = jnp.logical_and(depth < widths[j], lanes < widths[j])
        ends.append(squares(jnp.where(inside, child_inv[j], 0.0)))
    ends = jnp.concatenate(ends, axis=0)
    own = jnp.concatenate(
        [
            jnp.concatenate([level1[n, :, 128 * q : 128 * q + 128] for n in range(8)], axis=1)
            for q in range(4)
        ],
        axis=0,
    )
    lower = product(own, below_high, below_low)
    parity = lax.broadcasted_iota(jnp.int32, (64, 1024), 0) % 2
    parity_half = lax.broadcasted_iota(jnp.int32, (64, 256), 0) % 2
    for copy in cross_copies:
        copy.wait()
    lines = []
    for which in range(2):
        half = slice(256 * which, 256 * which + 256)
        known = jnp.concatenate(
            [cross[z, :, 128 * which : 128 * which + 128] for z in range(8)], axis=1
        )
        upper = image[:, half] - product(known, below_high[:, half], below_low[:, half])
        sums = squares(upper) + squares(jnp.where(parity_half == which, lower[:, half], 0.0))
        ends = ends + by_child(parents, which, sums)
        lines.append(squares(known) + squares(jnp.where(parity == which, own, 0.0)))
    for i in range(32):
        b = i // 4
        payload[i, 0:4, :] = ends
        payload[i, 4:5, :] = root[b, :, 128 * (i % 4) : 128 * (i % 4) + 128]
        payload[i, 5:6, :] = lines[0][:, 128 * b : 128 * b + 128]
        payload[i, 6:7, :] = lines[1][:, 128 * b : 128 * b + 128]
        payload[i, 7:8, :] = jnp.zeros((1, 128), f32)


def by_child(parents, which, sums):
    place = lax.broadcasted_iota(jnp.int32, (4, 128), 0)
    first, second = kids_in_order(parents)[2 * which : 2 * which + 2]
    return jnp.where(place == first, sums[:, :128], 0.0) + jnp.where(
        place == second, sums[:, 128:], 0.0
    )


def sum_kernel(ids, parts, root, parent, child):
    total = parts[0]
    for i in range(1, 32):
        total = total + parts[i]
    child[...] = total[0:4, :]
    root[...] = total[4:5, :]
    place = ids[2] % 4
    found = total[5:7, 0:32]
    for n in range(1, 4):
        found = jnp.where(place == n, total[5:7, 32 * n : 32 * n + 32], found)
    parent[...] = found


def moved(x, down, right):
    def target(i):
        y, x, core = i // 8, i // 2 % 4, i % 2
        return ((y + down) % 4 * 4 + (x + right) % 4) * 2 + core

    return lax.ppermute(x, "row", [(i, target(i)) for i in range(32)])


def along(x, n):
    return lax.ppermute(x, "col", [(z, (z + n) % 8) for z in range(8)])


def body(
    root_inv,
    level1_inv,
    level1_panel,
    child_inv,
    child_panel,
    child_width,
    child_parent,
    child_blocks,
):
    row = lax.axis_index("row")
    col = lax.axis_index("col")
    ids = jnp.stack([row & 1, col, row]).astype(jnp.int32)

    packed, panels, children = call(
        pack_kernel,
        [((144, 512), f32), ((16, 2, 128, 128), f32), ((16, 4, 64, 128), f32)],
        [VMEM] * 4, (0, 5_000_000),
    )(root_inv, level1_inv.reshape(64, 128), level1_panel.reshape(256, 128), child_panel)
    fence = lax.optimization_barrier
    down, up = [packed], [packed]
    for n in range(3):
        down.append(along(down[-1], 1))
        up.append(along(up[-1], -1))
    mine = lax.all_to_all(
        panels, "row", 0, 0, tiled=True, axis_index_groups=SAME_CORE
    )
    mine, children, down[3], up[3] = fence((mine, children, down[3], up[3]))
    rows = down + [along(down[3], 1)] + up[1:]
    panels = [mine, lax.ppermute(mine, "row", PAIRS)]
    mine = lax.all_to_all(
        children, "row", 0, 0, tiled=True, axis_index_groups=SAME_CORE
    )

    cross, root = call(
        cross_kernel, [((128, 256), f32), ((8, 1, 512), f32)],
        [SMEM] + [HBM] * 8 + [ANY, HBM], (40_000_000_000, 6_000_000),
        [
            pltpu.VMEM((8, 128, 512), f32),
            pltpu.VMEM((2, 16, 2, 128, 128), f32),
            pltpu.VMEM((256, 4096), bf16),
            pltpu.VMEM((4096, 256), bf16),
            pltpu.VMEM((4096, 256), bf16),
            pltpu.SemaphoreType.DMA((8,)),
            pltpu.SemaphoreType.DMA((2,)),
        ],
        32,
    )(ids, *rows, *panels)
    crosses = [along(cross, n) for n in (1, -1, 2, -2, 4)]
    crosses = [cross] + crosses + [along(crosses[2], 1), along(crosses[3], -1)]
    mine, _ = fence((mine, crosses))
    children = [mine, lax.ppermute(mine, "row", PAIRS)]

    (payload,) = call(
        child_kernel, [((32, 8, 128), f32)],
        [SMEM] * 4 + [VMEM] * 2 + [HBM] * 8 + [ANY, HBM] + [HBM] * 8,
        (2_000_000_000, 10_000_000),
        [
            pltpu.VMEM((8, 128, 512), f32),
            pltpu.VMEM((8, 16, 512), f32),
            pltpu.VMEM((2, 16, 4, 64, 128), f32),
            pltpu.VMEM((8, 128, 256), f32),
            pltpu.VMEM((256, 4096), bf16),
            pltpu.VMEM((5120, 512), bf16),
            pltpu.VMEM((5120, 512), bf16),
            pltpu.SemaphoreType.DMA((16,)),
            pltpu.SemaphoreType.DMA((2,)),
            pltpu.SemaphoreType.DMA((8,)),
        ],
        60,
    )(
        ids, child_parent, child_width, child_blocks, child_inv, root,
        *rows, *children, *crosses,
    )
    root, parent, child = call(
        sum_kernel, [((1, 128), f32), ((2, 32), f32), ((4, 128), f32)], [SMEM, VMEM],
        (0, 130_000), (), 16,
    )(ids, lax.all_to_all(payload, "row", 0, 0, tiled=True))
    return root.reshape(128), parent, child


def solution(mesh):
    placed = (
        P("row", "col"),
        P("row", None, "col"),
        P("row", None, "col"),
        P(None, "row", "col"),
        P(None, "row", "col"),
        P(),
        P(),
        P(),
    )
    return jax.shard_map(
        body,
        mesh=mesh,
        in_specs=placed,
        out_specs=(P("row"), P(None, "row"), P(None, "col")),
        check_vma=False,
    )
```

```python
import jax
import jax.numpy as jnp
from jax import lax
from jax.experimental import pallas as pl
from jax.experimental.pallas import tpu as pltpu
from jax.sharding import PartitionSpec as P

BLOCK_ROWS = 32
PAIRS = [(i, i ^ 1) for i in range(32)]
SAME_CORE = [[2 * m + k for m in range(16)] for k in range(2)]
f32 = jnp.float32
bf16 = jnp.bfloat16

VMEM = pl.BlockSpec(memory_space=pltpu.VMEM)
ANY = pl.BlockSpec(memory_space=pl.ANY)
HBM = pl.BlockSpec(memory_space=pltpu.HBM)
SMEM = pl.BlockSpec(memory_space=pltpu.SMEM)


def call(kernel, outs, ins, cost, scratch=(), mib=60):
    return pl.pallas_call(
        kernel,
        out_shape=[jax.ShapeDtypeStruct(*out) for out in outs],
        in_specs=ins,
        out_specs=[VMEM] * len(outs),
        scratch_shapes=list(scratch),
        compiler_params=pltpu.CompilerParams(vmem_limit_bytes=60 * 1024 * 1024),
        cost_estimate=pl.CostEstimate(flops=cost[0], bytes_accessed=cost[1], transcendentals=0),
    )


def split(x):
    high = x.astype(bf16)
    return high, (x - high.astype(f32)).astype(bf16)


def dot(a, b):
    return jnp.dot(a, b, preferred_element_type=f32)


def product(x, high, low):
    up, down = split(x)
    rows = x.shape[0]
    both = dot(jnp.concatenate([up, down], axis=0), high)
    return both[:rows] + both[rows:] + dot(up, low)


def squares(x):
    return jnp.sum(x * x, axis=0, keepdims=True)


def kids_in_order(parents):
    order = []
    for which in range(2):
        hit = [parents[j] == which for j in range(4)]
        order.append(jnp.where(hit[0], 0, jnp.where(hit[1], 1, 2)))
        order.append(jnp.where(hit[3], 3, jnp.where(hit[2], 2, 1)))
    return order


def pack_kernel(root_inv, level1, panel, child, out, panels, children):
    out[0:128, :] = root_inv[...]
    for which in range(2):
        apart = panel[pl.ds(which, 128, stride=2), :]
        for n in range(16):
            panels[n, which] = apart
    whole = child[...]
    for n in range(16):
        children[n] = whole
    for q in range(4):
        out[128:144, 128 * q : 128 * q + 128] = level1[16 * q : 16 * q + 16, :]


def chip_of(ids):
    return ids[2] // 8, (ids[2] // 2) % 4


def fetch_rows(ids, parts, factor, tail, arrived):
    copies = []
    for n, away in enumerate((0, 1, 2, 3, 4, 7, 6, 5)):
        z = (ids[1] + 8 - away) % 8
        copies.append(
            pltpu.make_async_copy(parts[n].at[pl.ds(0, 128)], factor.at[z], arrived.at[n])
        )
        if tail is not None:
            copies.append(
                pltpu.make_async_copy(
                    parts[n].at[pl.ds(128, 16)], tail.at[z], arrived.at[8 + n]
                )
            )
    return copies


def split_rows(copies, factor, both):
    for copy in copies:
        copy.wait()
    for z in range(8):
        high, low = split(factor[z])
        both[0:128, 512 * z : 512 * z + 512] = high
        both[128:256, 512 * z : 512 * z + 512] = low


def times_rows(both, high, low):
    first = dot(both[...], high)
    return first[:128] + first[128:] + dot(both[0:128, :], low)


def cross_kernel(ids, *refs):
    parts, sides, refs = refs[:8], refs[8:10], refs[10:]
    cross, root, factor, panels, both, high, low, row_here, panel_here = refs
    row_copies = fetch_rows(ids, parts, factor, None, row_here)
    copies = [
        pltpu.make_async_copy(side, panels.at[n], panel_here.at[n])
        for n, side in enumerate(sides)
    ]
    for copy in copies + row_copies:
        copy.start()
    for n, copy in enumerate(copies):
        copy.wait()
        core = ids[0] if n == 0 else 1 - ids[0]
        for chip in range(16):
            spot = pl.ds(pl.multiple_of(128 * (2 * chip + core), 128), 128)
            for which in range(2):
                up, down = split(panels[n, chip, which])
                high[spot, 128 * which : 128 * which + 128] = up
                low[spot, 128 * which : 128 * which + 128] = down
    split_rows(row_copies, factor, both)
    for z in range(8):
        root[z] = squares(factor[z])
    cross[...] = times_rows(both, high[...], low[...])


def child_kernel(ids, parents, widths, blocks, child_inv, root, *refs):
    rows, sides, parts, refs = refs[:8], refs[8:10], refs[10:18], refs[18:]
    payload, factor, level1, panels, cross, both, high, low = refs[:8]
    row_here, part_here, cross_here = refs[8:]
    cross_copies = [
        pltpu.make_async_copy(
            parts[n], cross.at[(ids[1] + 8 - away) % 8], cross_here.at[n]
        )
        for n, away in enumerate((0, 1, 7, 2, 6, 4, 3, 5))
    ]
    copies = [
        pltpu.make_async_copy(sides[0], panels, part_here.at[0])
    ]
    row_copies = fetch_rows(ids, rows, factor, level1, row_here)
    for copy in copies + row_copies + cross_copies:
        copy.start()
    high[...] = jnp.zeros_like(high)
    low[...] = jnp.zeros_like(low)
    lanes = ids[1] * 128 + lax.broadcasted_iota(jnp.int32, (32, 128), 1)
    order = kids_in_order(parents)
    live = [lanes < widths[kid] for kid in order]
    for n, side in enumerate((panels, sides[1])):
        if n == 0:
            copies[0].wait()
        core = ids[0] if n == 0 else 1 - ids[0]
        for chip in range(16):
            for half in range(2):
                slot = 4 * chip + 2 * core + half
                for place, kid in enumerate(order):
                    row = pl.multiple_of(blocks[kid, slot] * BLOCK_ROWS, BLOCK_ROWS)
                    piece = side[chip, kid, 32 * half : 32 * half + 32, :]
                    up, down = split(jnp.where(live[place], piece, 0.0))
                    high[pl.ds(row, 32), 128 * place : 128 * place + 128] = up
                    low[pl.ds(row, 32), 128 * place : 128 * place + 128] = down
    split_rows(row_copies, factor, both)
    image = times_rows(both, high[0:4096, :], low[0:4096, :])
    below_high, below_low = high[4096:5120, :], low[4096:5120, :]
    depth = ids[2] * 32 + lax.broadcasted_iota(jnp.int32, (32, 128), 0)
    ends = []
    for j in range(4):
        inside = jnp.logical_and(depth < widths[j], lanes < widths[j])
        ends.append(squares(jnp.where(inside, child_inv[j], 0.0)))
    ends = jnp.concatenate(ends, axis=0)
    own = jnp.concatenate(
        [
            jnp.concatenate([level1[n, :, 128 * q : 128 * q + 128] for n in range(8)], axis=1)
            for q in range(4)
        ],
        axis=0,
    )
    lower = product(own, below_high, below_low)
    parity = lax.broadcasted_iota(jnp.int32, (64, 1024), 0) % 2
    parity_half = lax.broadcasted_iota(jnp.int32, (64, 256), 0) % 2
    for copy in cross_copies:
        copy.wait()
    lines = []
    for which in range(2):
        half = slice(256 * which, 256 * which + 256)
        known = jnp.concatenate(
            [cross[z, :, 128 * which : 128 * which + 128] for z in range(8)], axis=1
        )
        upper = image[:, half] - product(known, below_high[:, half], below_low[:, half])
        sums = squares(upper) + squares(jnp.where(parity_half == which, lower[:, half], 0.0))
        ends = ends + by_child(parents, which, sums)
        lines.append(squares(known) + squares(jnp.where(parity == which, own, 0.0)))
    for i in range(32):
        b = i // 4
        payload[i, 0:4, :] = ends
        payload[i, 4:5, :] = root[b, :, 128 * (i % 4) : 128 * (i % 4) + 128]
        payload[i, 5:6, :] = lines[0][:, 128 * b : 128 * b + 128]
        payload[i, 6:7, :] = lines[1][:, 128 * b : 128 * b + 128]
        payload[i, 7:8, :] = jnp.zeros((1, 128), f32)


def by_child(parents, which, sums):
    place = lax.broadcasted_iota(jnp.int32, (4, 128), 0)
    first, second = kids_in_order(parents)[2 * which : 2 * which + 2]
    return jnp.where(place == first, sums[:, :128], 0.0) + jnp.where(
        place == second, sums[:, 128:], 0.0
    )


def sum_kernel(ids, parts, root, parent, child):
    total = parts[0]
    for i in range(1, 32):
        total = total + parts[i]
    child[...] = total[0:4, :]
    root[...] = total[4:5, :]
    place = ids[2] % 4
    found = total[5:7, 0:32]
    for n in range(1, 4):
        found = jnp.where(place == n, total[5:7, 32 * n : 32 * n + 32], found)
    parent[...] = found


def moved(x, down, right):
    def target(i):
        y, x, core = i // 8, i // 2 % 4, i % 2
        return ((y + down) % 4 * 4 + (x + right) % 4) * 2 + core

    return lax.ppermute(x, "row", [(i, target(i)) for i in range(32)])


def along(x, n):
    return lax.ppermute(x, "col", [(z, (z + n) % 8) for z in range(8)])


def body(
    root_inv,
    level1_inv,
    level1_panel,
    child_inv,
    child_panel,
    child_width,
    child_parent,
    child_blocks,
):
    row = lax.axis_index("row")
    col = lax.axis_index("col")
    ids = jnp.stack([row & 1, col, row]).astype(jnp.int32)

    packed, panels, children = call(
        pack_kernel,
        [((144, 512), f32), ((16, 2, 128, 128), f32), ((16, 4, 64, 128), f32)],
        [VMEM] * 4, (0, 5_000_000),
    )(root_inv, level1_inv.reshape(64, 128), level1_panel.reshape(256, 128), child_panel)
    fence = lax.optimization_barrier
    down, up = [packed], [packed]
    for n in range(3):
        down.append(along(down[-1], 1))
        up.append(along(up[-1], -1))
    mine = lax.all_to_all(
        panels, "row", 0, 0, tiled=True, axis_index_groups=SAME_CORE
    )
    mine, children, down[3], up[3] = fence((mine, children, down[3], up[3]))
    rows = down + [along(down[3], 1)] + up[1:]
    panels = [mine, lax.ppermute(mine, "row", PAIRS)]
    mine = lax.all_to_all(
        children, "row", 0, 0, tiled=True, axis_index_groups=SAME_CORE
    )

    cross, root = call(
        cross_kernel, [((128, 256), f32), ((8, 1, 512), f32)],
        [SMEM] + [HBM] * 8 + [ANY, HBM], (40_000_000_000, 6_000_000),
        [
            pltpu.VMEM((8, 128, 512), f32),
            pltpu.VMEM((2, 16, 2, 128, 128), f32),
            pltpu.VMEM((256, 4096), bf16),
            pltpu.VMEM((4096, 256), bf16),
            pltpu.VMEM((4096, 256), bf16),
            pltpu.SemaphoreType.DMA((8,)),
            pltpu.SemaphoreType.DMA((2,)),
        ],
        32,
    )(ids, *rows, *panels)
    crosses = [along(cross, n) for n in (1, -1, 2, -2, 4)]
    crosses = [cross] + crosses + [along(crosses[2], 1), along(crosses[3], -1)]
    mine, _ = fence((mine, crosses))
    children = [mine, lax.ppermute(mine, "row", PAIRS)]

    (payload,) = call(
        child_kernel, [((32, 8, 128), f32)],
        [SMEM] * 4 + [VMEM] * 2 + [HBM] * 8 + [ANY, VMEM] + [HBM] * 8,
        (2_000_000_000, 10_000_000),
        [
            pltpu.VMEM((8, 128, 512), f32),
            pltpu.VMEM((8, 16, 512), f32),
            pltpu.VMEM((16, 4, 64, 128), f32),
            pltpu.VMEM((8, 128, 256), f32),
            pltpu.VMEM((256, 4096), bf16),
            pltpu.VMEM((5120, 512), bf16),
            pltpu.VMEM((5120, 512), bf16),
            pltpu.SemaphoreType.DMA((16,)),
            pltpu.SemaphoreType.DMA((1,)),
            pltpu.SemaphoreType.DMA((8,)),
        ],
        28,
    )(
        ids, child_parent, child_width, child_blocks, child_inv, root,
        *rows, *children, *crosses,
    )
    root, parent, child = call(
        sum_kernel, [((1, 128), f32), ((2, 32), f32), ((4, 128), f32)], [SMEM, VMEM],
        (0, 130_000), (), 16,
    )(ids, lax.all_to_all(payload, "row", 0, 0, tiled=True))
    return root.reshape(128), parent, child


def solution(mesh):
    placed = (
        P("row", "col"),
        P("row", None, "col"),
        P("row", None, "col"),
        P(None, "row", "col"),
        P(None, "row", "col"),
        P(),
        P(),
        P(),
    )
    return jax.shard_map(
        body,
        mesh=mesh,
        in_specs=placed,
        out_specs=(P("row"), P(None, "row"), P(None, "col")),
        check_vma=False,
    )
```
